32 devices in a mesh: dp: 8 (over y, x, core), mp: 4 (over z).
Axes of the slice: x: 2, y: 2, z: 4, core: 2. Of those that a mesh axis runs over, the one named last changes fastest.
Arguments:
- query_heads: bfloat16 [4096, 3072], P('dp', 'mp'), may hold values from -48 to 48
- key_heads: bfloat16 [4096, 3072], P('dp', 'mp'), may hold values from -8 to 8
- value_heads: bfloat16 [4096, 3072], P('dp', 'mp'), may hold values from -6 to 6
- upstream: bfloat16 [4096, 3072], P('dp', 'mp'), may hold values from -6 to 6
- out_weight: bfloat16 [3072, 3072], P('dp', 'mp'), may hold values from -0.109375 to 0.109375
Outputs:
- grad_query: bfloat16 [4096, 3072], P('dp', 'mp')
- grad_key: bfloat16 [4096, 3072], P('dp', 'mp')
- grad_value: bfloat16 [4096, 3072], P('dp', 'mp')
- grad_weight: float32 [3072, 3072], P('dp', 'mp')
The draws below stay inside these ranges and needn't reach their ends.
All inputs are finite; a program needn't handle non-finite values.
Results may differ from the reference program's by a relative error of at most 0.006.
Values may be sent and summed in bfloat16 or wider, within the bound.
A program may use at most 64 MiB of HBM per device.

```python
import jax
import jax.numpy as jnp
from jax import lax

D = 3072
HEAD = 128
PATCHES = 256
HD = 3072
IMAGES = 16
TOKENS = 4096


def draw_query_heads(key, part):
    key = jax.random.fold_in(key, 5)
    result = jnp.clip(jax.random.normal(key, (TOKENS, HD), jnp.float32), -6.0, 6.0)
    return result.astype(jnp.bfloat16)


def draw_key_heads(key, part):
    key = jax.random.fold_in(key, 9)
    result = jnp.clip(jax.random.normal(key, (TOKENS, HD), jnp.float32), -6.0, 6.0)
    return result.astype(jnp.bfloat16)


def with_spikes(drawn, key, source, target, shards_of, factor):
    owner, partner = [(jnp.arange(drawn.shape[dim]) // (drawn.shape[dim] // shards_of)).reshape([-1 if axis == dim else 1 for axis in range(drawn.ndim)]) for dim in (source, target)]
    chosen = jax.random.permutation(key, shards_of)[partner]
    strong = (owner == chosen) | (owner == (partner + shards_of // 2) % shards_of)
    return jnp.where(strong, factor * drawn, drawn)


def level_of(rng, shape, pieces, least, top_value):
    level, own = 1.0, jax.random.fold_in(rng, 6)
    for axis_at, blocks in pieces:
        heights = jnp.exp(jax.random.uniform(jax.random.fold_in(own, axis_at), (blocks,), jnp.float32, least / len(pieces), top_value / len(pieces)))
        level = level * jnp.repeat(heights, shape[axis_at] // blocks).reshape([-1 if axis == axis_at else 1 for axis in range(len(shape))])
    return level


def gaussian(rng, extent, spread, most, cuts=(), kind=jnp.bfloat16):
    level = level_of(rng, extent, cuts, -0.22, 0.18) if cuts else 1.0
    array = jax.random.normal(rng, extent, jnp.float32) * spread * level
    return jnp.minimum(jnp.maximum(array, -most), most).astype(kind)


def heavy_noise(key, dims, width, limit, cuts, heavy, kind=jnp.bfloat16):
    values = width * jax.random.normal(key, dims, jnp.float32)
    if cuts:
        values = values * level_of(key, dims, cuts, -0.22, 0.18)
    return jnp.clip(with_spikes(values, jax.random.fold_in(key, 3), *heavy), -limit, limit).astype(kind)


def setup_inputs(seed: int = 0) -> dict:
    arg_keys = jax.random.split(jax.random.key(seed), 6)
    return {
        "query_heads": draw_query_heads(jax.random.fold_in(arg_keys[5], 71), 0),
        "key_heads": draw_key_heads(jax.random.fold_in(arg_keys[5], 71), 0),
        "value_heads": gaussian(arg_keys[2], (TOKENS, HD), 1.0, 6.0, ((0, 8), (1, 4))),
        "upstream": heavy_noise(arg_keys[3], (TOKENS, D), 1.0, 6.0, ((0, 8), (1, 4)), (0, 1, 8, 2.0)),
        "out_weight": gaussian(arg_keys[4], (D, HD), D ** -0.5, 0.109375, ((0, 8), (1, 4))),
    }


def to_heads(tensor):
    return tensor.astype(jnp.float32).reshape(tensor.shape[0], -1, HEAD)


def from_heads(tensor):
    return tensor.reshape(tensor.shape[0], -1).astype(jnp.bfloat16)


def round_trip(tensor):
    return lax.optimization_barrier(tensor.astype(jnp.bfloat16)).astype(jnp.float32)


def one_image(blocks):
    query_full, key_full, value_full, context_grad = (to_heads(member) for member in blocks)
    scaling = HEAD ** -0.5
    scores = jnp.einsum("qhd,khd->hqk", query_full, key_full) * scaling
    attention = jax.nn.softmax(scores, axis=-1)
    weights_bf = round_trip(attention)
    context = from_heads(jnp.einsum("hqk,khd->qhd", weights_bf, value_full))
    grad_value = from_heads(jnp.einsum("hqk,qhd->khd", weights_bf, context_grad))
    grad_attention = jnp.einsum("qhd,khd->hqk", context_grad, value_full)
    centred = jnp.sum(attention * grad_attention, axis=-1, keepdims=True)
    grad_scores = round_trip(attention * (grad_attention - centred) * scaling)
    grad_query = from_heads(jnp.einsum("hqk,khd->qhd", grad_scores, key_full))
    grad_key = from_heads(jnp.einsum("hqk,qhd->khd", grad_scores, query_full))
    return grad_query, grad_key, grad_value, context


def reference(query_heads, key_heads, value_heads, upstream, out_weight):
    grad_context = jnp.dot(upstream, out_weight, preferred_element_type=jnp.float32).astype(jnp.bfloat16)
    stacked = tuple(member.reshape(IMAGES, PATCHES, HD) for member in (query_heads, key_heads, value_heads, grad_context))
    grad_query, grad_key, grad_value, context = lax.map(one_image, stacked)
    grad_weight = lax.dot_general(upstream, context.reshape(TOKENS, HD), (((0,), (0,)), ((), ())), preferred_element_type=jnp.float32)
    return grad_query.reshape(TOKENS, HD), grad_key.reshape(TOKENS, HD), grad_value.reshape(TOKENS, HD), grad_weight
```

```python
import jax
import jax.numpy as jnp
from jax import lax
from jax.experimental import pallas as pl
from jax.experimental.pallas import tpu as pltpu
from jax.sharding import PartitionSpec as P

HEAD = 128
PATCHES = 256


def shards(query_heads, key_heads, value_heads, upstream, out_weight):
    tokens_here = query_heads.shape[0]
    local_width = query_heads.shape[1]
    upstream_full = lax.all_gather(upstream, "mp", axis=1, tiled=True)
    columns = upstream_full
    context_sum = jnp.dot(
        columns,
        lax.all_gather(out_weight, "dp", axis=0, tiled=True),
        preferred_element_type=jnp.float32,
    )
    grad_context = context_sum.astype(jnp.bfloat16)
    images_here = tokens_here // PATCHES
    scaling = HEAD ** (-0.5)

    def heads_of(tensor):
        return tensor.reshape(images_here, PATCHES, -1, HEAD)

    def rows_of(tensor):
        return tensor.reshape(tokens_here, local_width).astype(jnp.bfloat16)

    query_split = heads_of(query_heads)
    key_split = heads_of(key_heads)
    value_split = heads_of(value_heads)
    context_split = heads_of(grad_context)
    scores = (
        jnp.einsum("bqhd,bkhd->bhqk", query_split, key_split, preferred_element_type=jnp.float32)
        * scaling
    )
    attention = jax.nn.softmax(scores, axis=-1)
    weights_bf = attention.astype(jnp.bfloat16)
    context = rows_of(
        jnp.einsum("bhqk,bkhd->bqhd", weights_bf, value_split, preferred_element_type=jnp.float32)
    )
    columns = upstream_full
    grad_weight = lax.psum_scatter(
        lax.dot_general(
            columns, context, (((0,), (0,)), ((), ())), preferred_element_type=jnp.float32
        ),
        "dp",
        scatter_dimension=0,
        tiled=True,
    )
    grad_value = rows_of(
        jnp.einsum("bhqk,bqhd->bkhd", weights_bf, context_split, preferred_element_type=jnp.float32)
    )
    grad_attention = jnp.einsum(
        "bqhd,bkhd->bhqk", context_split, value_split, preferred_element_type=jnp.float32
    )
    centred = jnp.sum(attention * grad_attention, axis=-1, keepdims=True)
    grad_scores = (attention * (grad_attention - centred) * scaling).astype(jnp.bfloat16)
    grad_query = rows_of(
        jnp.einsum("bhqk,bkhd->bqhd", grad_scores, key_split, preferred_element_type=jnp.float32)
    )
    grad_key = rows_of(
        jnp.einsum("bhqk,bqhd->bkhd", grad_scores, query_split, preferred_element_type=jnp.float32)
    )
    return (grad_query, grad_key, grad_value, grad_weight)


MESH = pl.DeviceIdType.MESH
PLANES = 4
CHIPS = 4
PIECES = 3
PIECE = 128


def dot(left, right, left_dim, right_dim):
    return lax.dot_general(
        left, right, (((left_dim,), (right_dim,)), ((), ())), preferred_element_type=jnp.float32
    )


def fused_kernel(
    q_ref, k_ref, v_ref, u_ref, w_ref,
    gq_ref, gk_ref, gv_ref, gw_ref,
    u_all, w_all, attention, context, grad_context, partial, pair_out, pair_in, sum_out, sum_in,
    up_send, down_send, u_recv, pair_send, pair_recv, sum_send, sum_recv, w_send, w_recv,
):
    rank = lax.axis_index("dp")
    plane = lax.axis_index("mp")
    chip, core = rank // 2, rank % 2
    sibling = rank + 1 - 2 * core
    tokens, width = q_ref.shape
    heads = width // HEAD
    images = tokens // PATCHES
    scaling = HEAD ** (-0.5)
    chips_at = (chip, chip + 1 - 2 * (chip % 2), chip + 2 - 4 * (chip // 2), 3 - chip)

    def at(rank_there, plane_there):
        return {"dp": rank_there, "mp": plane_there}

    barrier = pltpu.get_barrier_semaphore()
    for rank_there in (sibling,) + tuple(2 * other + core for other in chips_at[1:]):
        pl.semaphore_signal(barrier, inc=1, device_id=at(rank_there, plane), device_id_type=MESH)
    for plane_there in ((plane + 1) % PLANES, (plane + PLANES - 1) % PLANES):
        pl.semaphore_signal(barrier, inc=1, device_id=at(rank, plane_there), device_id_type=MESH)

    for piece in range(PIECES):
        for half in range(2):
            u_all[plane, piece, :, half * PIECE : (half + 1) * PIECE] = u_ref[
                :, (half * PIECES + piece) * PIECE : (half * PIECES + piece + 1) * PIECE
            ]

    pl.semaphore_wait(barrier, 6)

    def remote(src, dst, send, recv, rank_there, plane_there):
        return pltpu.make_async_remote_copy(
            src_ref=src, dst_ref=dst, send_sem=send, recv_sem=recv,
            device_id=at(rank_there, plane_there), device_id_type=MESH,
        )

    def up_copy(shard, piece):
        block = u_all.at[shard, piece]
        return remote(
            block, block, up_send.at[shard, piece], u_recv.at[shard, piece], rank,
            (plane + 1) % PLANES,
        )

    def down_copy(shard, piece):
        block = u_all.at[shard, piece]
        return remote(
            block, block, down_send.at[shard, piece], u_recv.at[shard, piece], rank,
            (plane + PLANES - 1) % PLANES,
        )

    def goes_up(shard):
        return (plane < PLANES - 1) & (shard <= plane)

    def goes_down(shard):
        return (plane > 0) & (shard >= plane)

    def send_on(shard, piece):
        @pl.when(goes_up(shard))
        def _():
            up_copy(shard, piece).start()

        @pl.when(goes_down(shard))
        def _():
            down_copy(shard, piece).start()

    send_on(plane, 0)

    def w_copy(step):
        if step == 0:
            return remote(
                w_ref, w_all.at[chip, :, core], w_send.at[0], w_recv.at[0], sibling, plane
            )
        return remote(
            w_ref, w_all.at[chip, :, core], w_send.at[step], w_recv.at[step],
            2 * chips_at[step] + core, plane,
        )

    def w_forward(step):
        block = w_all.at[chips_at[step], :, core]
        return remote(block, block, w_send.at[3 + step], w_recv.at[3 + step], sibling, plane)

    for step in (1, 2, 3, 0):
        w_copy(step).start()
    send_on(plane, 1)
    for piece in range(PIECES):
        w_all[chip, piece, core] = w_ref[piece]

    def rows_columns(index):
        rows = pl.ds(pl.multiple_of((index // heads) * PATCHES, PATCHES), PATCHES)
        columns = pl.ds(pl.multiple_of((index % heads) * HEAD, HEAD), HEAD)
        return rows, columns

    def forward(index, carry):
        rows, columns = rows_columns(index)
        scores = dot(q_ref[rows, columns], k_ref[rows, columns], 1, 1) * scaling
        raised = jnp.exp(scores - jnp.max(scores, axis=-1, keepdims=True))
        weights = raised / jnp.sum(raised, axis=-1, keepdims=True)
        attention[index] = weights
        context[rows, columns] = dot(
            weights.astype(jnp.bfloat16), v_ref[rows, columns], 1, 0
        ).astype(jnp.bfloat16)
        return carry

    lax.fori_loop(0, images * heads, forward, 0)
    grad_context[...] = jnp.zeros_like(grad_context)

    def pair_copy(shard, piece):
        return remote(
            pair_out.at[shard, piece], pair_in.at[shard, piece], pair_send.at[shard, piece],
            pair_recv.at[shard, piece], sibling, plane,
        )

    def sum_copy(shard, piece):
        return remote(
            sum_out.at[shard, piece], sum_in.at[chip, piece], sum_send.at[shard, piece],
            sum_recv.at[chip, piece], 2 * shard + core, plane,
        )

    def shard_of(order):
        distance = (order + 1) // 2
        shard = plane + distance * (1 - 2 * (order % 2))
        return shard, (shard >= 0) & (shard < PLANES)

    def finish(order, piece):
        shard, valid = shard_of(order)

        @pl.when(valid)
        def _():
            pair_copy(shard, piece).wait_recv()

            @pl.when(shard == chip)
            def _():
                partial[shard, piece, core] += pair_in[shard, piece].astype(jnp.float32)

            @pl.when(shard != chip)
            def _():
                total = partial[shard, piece, core] + pair_in[shard, piece].astype(jnp.float32)
                sum_out[shard, piece] = total.astype(jnp.bfloat16)
                sum_copy(shard, piece).start()

    def visit(order, piece, last):
        shard, valid = shard_of(order)

        @pl.when(valid)
        def _():
            @pl.when(order > 0)
            def _():
                up_copy(shard, piece).wait_recv()
                send_on(shard, piece)

        @pl.when(order > 0)
        def _():
            finish(order - 1, piece)

        @pl.when(valid)
        def _():
            for tile in range(width // 256):
                columns = slice(tile * 256, (tile + 1) * 256)
                product = dot(u_all[shard, piece], context[:, columns], 0, 0)
                partial[shard, piece, :, :, columns] = product.reshape(2, PIECE, 256)
            pair_out[shard, piece] = partial[shard, piece, 1 - core].astype(jnp.bfloat16)
            pair_copy(shard, piece).start()
            if last:
                def tile_of(tile, carry):
                    columns = pl.ds(pl.multiple_of(tile * 256, 256), 256)
                    total = grad_context[:, columns]
                    for part in range(PIECES):
                        rows = w_all[shard, part, :, :, columns].reshape(2 * PIECE, 256)
                        total += dot(u_all[shard, part], rows, 1, 0)
                    grad_context[:, columns] = total
                    return carry

                lax.fori_loop(0, width // 256, tile_of, 0)

    orders = 2 * PLANES - 1
    for piece in range(PIECES):
        if piece == PIECES - 1:
            for step in (1, 2, 3):
                w_copy(step).wait_recv()
                w_forward(step).start()
            w_copy(0).wait_recv()
            for step in (1, 2, 3):
                w_forward(step).wait_recv()

        def step_of(order, carry, piece=piece):
            visit(order, piece, piece == PIECES - 1)
            return carry

        lax.fori_loop(0, orders, step_of, 0)
        if piece + 2 < PIECES:
            send_on(plane, piece + 2)
        finish(orders - 1, piece)

    def backward(index, carry):
        rows, columns = rows_columns(index)
        weights = attention[index]
        weights_bf = weights.astype(jnp.bfloat16)
        context_grad = grad_context[rows, columns].astype(jnp.bfloat16)
        gv_ref[rows, columns] = dot(weights_bf, context_grad, 0, 0).astype(jnp.bfloat16)
        attention_grad = dot(context_grad, v_ref[rows, columns], 1, 1)
        centred = jnp.sum(weights * attention_grad, axis=-1, keepdims=True)
        scores_grad = (weights * (attention_grad - centred) * scaling).astype(jnp.bfloat16)
        gq_ref[rows, columns] = dot(scores_grad, k_ref[rows, columns], 1, 0).astype(jnp.bfloat16)
        gk_ref[rows, columns] = dot(scores_grad, q_ref[rows, columns], 0, 0).astype(jnp.bfloat16)
        return carry

    lax.fori_loop(0, images * heads, backward, 0)

    for piece in range(PIECES):
        total = partial[chip, piece, core]
        for other in chips_at[1:]:
            block = sum_in.at[other, piece]
            remote(
                block, block, sum_send.at[other, piece], sum_recv.at[other, piece],
                2 * other + core, plane,
            ).wait_recv()
            total += sum_in[other, piece].astype(jnp.float32)
        gw_ref[piece * PIECE : (piece + 1) * PIECE, :] = total

    for step in range(4):
        w_copy(step).wait_send()
        if step:
            w_forward(step).wait_send()

    def drain(index, carry):
        shard, piece = index // PIECES, index % PIECES
        pair_copy(shard, piece).wait_send()

        @pl.when(shard != chip)
        def _():
            sum_copy(shard, piece).wait_send()

        @pl.when(goes_up(shard))
        def _():
            up_copy(shard, piece).wait_send()

        @pl.when(goes_down(shard))
        def _():
            down_copy(shard, piece).wait_send()

        return carry

    lax.fori_loop(0, PLANES * PIECES, drain, 0)


def fused_shards(query_heads, key_heads, value_heads, upstream, out_weight):
    tokens, width = query_heads.shape
    rows = out_weight.shape[0]
    heads = (tokens // PATCHES) * (width // HEAD)
    bf16, f32 = jnp.bfloat16, jnp.float32
    many = pltpu.SemaphoreType.DMA((PLANES, PIECES))
    few = pltpu.SemaphoreType.DMA((7,))
    piece_of = (PLANES, PIECES, PIECE, width)
    vmem = pl.BlockSpec(memory_space=pltpu.VMEM)
    return pl.pallas_call(
        fused_kernel,
        out_shape=[jax.ShapeDtypeStruct((tokens, width), bf16)] * 3
        + [jax.ShapeDtypeStruct((rows, width), f32)],
        in_specs=[vmem] * 5,
        out_specs=[vmem] * 4,
        scratch_shapes=[
            pltpu.VMEM((PLANES, PIECES, tokens, 2 * PIECE), bf16),
            pltpu.VMEM((CHIPS, PIECES, 2, PIECE, width), bf16),
            pltpu.VMEM((heads, PATCHES, PATCHES), f32),
            pltpu.VMEM((tokens, width), bf16),
            pltpu.VMEM((tokens, width), f32),
            pltpu.VMEM((PLANES, PIECES, 2, PIECE, width), f32),
            pltpu.VMEM(piece_of, bf16),
            pltpu.VMEM(piece_of, bf16),
            pltpu.VMEM(piece_of, bf16),
            pltpu.VMEM(piece_of, bf16),
        ]
        + [many] * 7
        + [few] * 2,
        compiler_params=pltpu.CompilerParams(
            collective_id=0, has_side_effects=True, vmem_limit_bytes=56 * 2**20
        ),
        cost_estimate=pl.CostEstimate(
            flops=6_000_000_000, bytes_accessed=8_000_000, transcendentals=786_432
        ),
        name="fused",
    )(
        query_heads, key_heads, value_heads, upstream,
        out_weight.reshape(PIECES, PIECE, width),
    )


def solution(mesh):
    fits = mesh.shape["dp"] == 2 * CHIPS and mesh.shape["mp"] == PLANES
    return jax.shard_map(
        fused_shards if fits else shards,
        mesh=mesh,
        in_specs=(P("dp", "mp"), P("dp", "mp"), P("dp", "mp"), P("dp", "mp"), P("dp", "mp")),
        out_specs=(P("dp", "mp"), P("dp", "mp"), P("dp", "mp"), P("dp", "mp")),
        check_vma=False,
    )
```

```python
import jax
import jax.numpy as jnp
from jax import lax
from jax.experimental import pallas as pl
from jax.experimental.pallas import tpu as pltpu
from jax.sharding import PartitionSpec as P

HEAD = 128
PATCHES = 256


def shards(query_heads, key_heads, value_heads, upstream, out_weight):
    tokens_here = query_heads.shape[0]
    local_width = query_heads.shape[1]
    upstream_full = lax.all_gather(upstream, "mp", axis=1, tiled=True)
    columns = upstream_full
    context_sum = jnp.dot(
        columns,
        lax.all_gather(out_weight, "dp", axis=0, tiled=True),
        preferred_element_type=jnp.float32,
    )
    grad_context = context_sum.astype(jnp.bfloat16)
    images_here = tokens_here // PATCHES
    scaling = HEAD ** (-0.5)

    def heads_of(tensor):
        return tensor.reshape(images_here, PATCHES, -1, HEAD)

    def rows_of(tensor):
        return tensor.reshape(tokens_here, local_width).astype(jnp.bfloat16)

    query_split = heads_of(query_heads)
    key_split = heads_of(key_heads)
    value_split = heads_of(value_heads)
    context_split = heads_of(grad_context)
    scores = (
        jnp.einsum("bqhd,bkhd->bhqk", query_split, key_split, preferred_element_type=jnp.float32)
        * scaling
    )
    attention = jax.nn.softmax(scores, axis=-1)
    weights_bf = attention.astype(jnp.bfloat16)
    context = rows_of(
        jnp.einsum("bhqk,bkhd->bqhd", weights_bf, value_split, preferred_element_type=jnp.float32)
    )
    columns = upstream_full
    grad_weight = lax.psum_scatter(
        lax.dot_general(
            columns, context, (((0,), (0,)), ((), ())), preferred_element_type=jnp.float32
        ),
        "dp",
        scatter_dimension=0,
        tiled=True,
    )
    grad_value = rows_of(
        jnp.einsum("bhqk,bqhd->bkhd", weights_bf, context_split, preferred_element_type=jnp.float32)
    )
    grad_attention = jnp.einsum(
        "bqhd,bkhd->bhqk", context_split, value_split, preferred_element_type=jnp.float32
    )
    centred = jnp.sum(attention * grad_attention, axis=-1, keepdims=True)
    grad_scores = (attention * (grad_attention - centred) * scaling).astype(jnp.bfloat16)
    grad_query = rows_of(
        jnp.einsum("bhqk,bkhd->bqhd", grad_scores, key_split, preferred_element_type=jnp.float32)
    )
    grad_key = rows_of(
        jnp.einsum("bhqk,bqhd->bkhd", grad_scores, query_split, preferred_element_type=jnp.float32)
    )
    return (grad_query, grad_key, grad_value, grad_weight)


MESH = pl.DeviceIdType.MESH
PLANES = 4
CHIPS = 4
PIECES = 3
PIECE = 128


def dot(left, right, left_dim, right_dim):
    return lax.dot_general(
        left, right, (((left_dim,), (right_dim,)), ((), ())), preferred_element_type=jnp.float32
    )


def fused_kernel(
    q_hbm, k_hbm, v_hbm, u_hbm, w_hbm,
    gq_hbm, gk_hbm, gv_hbm, gw_hbm,
    q_ref, k_ref, v_ref, gq_ref, gk_ref, gv_ref, gw_ref,
    u_all, w_all, attention, context, grad_context, partial, pair_out, pair_in, sum_out, sum_in,
    up_send, down_send, u_recv, pair_send, pair_recv, sum_send, sum_recv, w_send, w_recv, u_load, load, store,
):
    rank = lax.axis_index("dp")
    plane = lax.axis_index("mp")
    chip, core = rank // 2, rank % 2
    sibling = rank + 1 - 2 * core
    tokens, width = q_ref.shape
    heads = width // HEAD
    images = tokens // PATCHES
    scaling = HEAD ** (-0.5)
    chips_at = (chip, chip + 1 - 2 * (chip % 2), chip + 2 - 4 * (chip // 2), 3 - chip)

    def at(rank_there, plane_there):
        return {"dp": rank_there, "mp": plane_there}

    barrier = pltpu.get_barrier_semaphore()
    for rank_there in (sibling,) + tuple(2 * other + core for other in chips_at[1:]):
        pl.semaphore_signal(barrier, inc=1, device_id=at(rank_there, plane), device_id_type=MESH)
    for plane_there in ((plane + 1) % PLANES, (plane + PLANES - 1) % PLANES):
        pl.semaphore_signal(barrier, inc=1, device_id=at(rank, plane_there), device_id_type=MESH)

    def u_loads(piece):
        return [
            pltpu.make_async_copy(
                u_hbm.at[:, pl.ds((half * PIECES + piece) * PIECE, PIECE)],
                u_all.at[plane, piece, :, pl.ds(half * PIECE, PIECE)],
                u_load.at[piece, half],
            )
            for half in range(2)
        ]

    loads = [
        pltpu.make_async_copy(q_hbm, q_ref, load.at[0]),
        pltpu.make_async_copy(k_hbm, k_ref, load.at[1]),
        pltpu.make_async_copy(v_hbm, v_ref, load.at[2]),
        pltpu.make_async_copy(w_hbm, w_all.at[chip, :, core], load.at[3]),
    ]
    for piece in range(PIECES):
        for copy in u_loads(piece):
            copy.start()
    for copy in loads:
        copy.start()
    pl.semaphore_wait(barrier, 6)

    def remote(src, dst, send, recv, rank_there, plane_there):
        return pltpu.make_async_remote_copy(
            src_ref=src, dst_ref=dst, send_sem=send, recv_sem=recv,
            device_id=at(rank_there, plane_there), device_id_type=MESH,
        )

    def up_copy(shard, piece):
        block = u_all.at[shard, piece]
        return remote(
            block, block, up_send.at[shard, piece], u_recv.at[shard, piece], rank,
            (plane + 1) % PLANES,
        )

    def down_copy(shard, piece):
        block = u_all.at[shard, piece]
        return remote(
            block, block, down_send.at[shard, piece], u_recv.at[shard, piece], rank,
            (plane + PLANES - 1) % PLANES,
        )

    def goes_up(shard):
        return (plane < PLANES - 1) & (shard <= plane)

    def goes_down(shard):
        return (plane > 0) & (shard >= plane)

    def send_on(shard, piece):
        @pl.when(goes_up(shard))
        def _():
            up_copy(shard, piece).start()

        @pl.when(goes_down(shard))
        def _():
            down_copy(shard, piece).start()

    for copy in u_loads(0):
        copy.wait()
    send_on(plane, 0)

    def w_copy(step):
        if step == 0:
            return remote(
                w_hbm, w_all.at[chip, :, core], w_send.at[0], w_recv.at[0], sibling, plane
            )
        return remote(
            w_hbm, w_all.at[chip, :, core], w_send.at[step], w_recv.at[step],
            2 * chips_at[step] + core, plane,
        )

    def w_forward(step):
        block = w_all.at[chips_at[step], :, core]
        return remote(block, block, w_send.at[3 + step], w_recv.at[3 + step], sibling, plane)

    for step in (1, 2, 3, 0):
        w_copy(step).start()
    for piece in range(1, PIECES):
        for copy in u_loads(piece):
            copy.wait()
        send_on(plane, piece)
    for copy in loads:
        copy.wait()

    def rows_columns(index):
        rows = pl.ds(pl.multiple_of((index // heads) * PATCHES, PATCHES), PATCHES)
        columns = pl.ds(pl.multiple_of((index % heads) * HEAD, HEAD), HEAD)
        return rows, columns

    def forward(index, carry):
        rows, columns = rows_columns(index)
        scores = dot(q_ref[rows, columns], k_ref[rows, columns], 1, 1) * scaling
        raised = jnp.exp(scores - jnp.max(scores, axis=-1, keepdims=True))
        weights = raised / jnp.sum(raised, axis=-1, keepdims=True)
        attention[index] = weights
        context[rows, columns] = dot(
            weights.astype(jnp.bfloat16), v_ref[rows, columns], 1, 0
        ).astype(jnp.bfloat16)
        return carry

    lax.fori_loop(0, images * heads, forward, 0)
    grad_context[...] = jnp.zeros_like(grad_context)

    def pair_copy(shard, piece):
        return remote(
            pair_out.at[shard, piece], pair_in.at[shard, piece], pair_send.at[shard, piece],
            pair_recv.at[shard, piece], sibling, plane,
        )

    def sum_copy(shard, piece):
        return remote(
            sum_out.at[shard, piece], sum_in.at[chip, piece], sum_send.at[shard, piece],
            sum_recv.at[chip, piece], 2 * shard + core, plane,
        )

    def shard_of(order):
        distance = (order + 1) // 2
        shard = plane + distance * (1 - 2 * (order % 2))
        return shard, (shard >= 0) & (shard < PLANES)

    def finish(order, piece):
        shard, valid = shard_of(order)

        @pl.when(valid)
        def _():
            pair_copy(shard, piece).wait_recv()

            @pl.when(shard == chip)
            def _():
                partial[shard, piece, core] += pair_in[shard, piece].astype(jnp.float32)

            @pl.when(shard != chip)
            def _():
                total = partial[shard, piece, core] + pair_in[shard, piece].astype(jnp.float32)
                sum_out[shard, piece] = total.astype(jnp.bfloat16)
                sum_copy(shard, piece).start()

    def visit(order, piece, last):
        shard, valid = shard_of(order)

        @pl.when(valid)
        def _():
            @pl.when(order > 0)
            def _():
                up_copy(shard, piece).wait_recv()
                send_on(shard, piece)

        @pl.when(order > 0)
        def _():
            finish(order - 1, piece)

        @pl.when(valid)
        def _():
            for tile in range(width // 256):
                columns = slice(tile * 256, (tile + 1) * 256)
                product = dot(u_all[shard, piece], context[:, columns], 0, 0)
                partial[shard, piece, :, :, columns] = product.reshape(2, PIECE, 256)
            pair_out[shard, piece] = partial[shard, piece, 1 - core].astype(jnp.bfloat16)
            pair_copy(shard, piece).start()
            if last:
                def tile_of(tile, carry):
                    columns = pl.ds(pl.multiple_of(tile * 256, 256), 256)
                    total = grad_context[:, columns]
                    for part in range(PIECES):
                        rows = w_all[shard, part, :, :, columns].reshape(2 * PIECE, 256)
                        total += dot(u_all[shard, part], rows, 1, 0)
                    grad_context[:, columns] = total
                    return carry

                lax.fori_loop(0, width // 256, tile_of, 0)

    orders = 2 * PLANES - 1
    for piece in range(PIECES):
        if piece == PIECES - 1:
            for step in (1, 2, 3):
                w_copy(step).wait_recv()
                w_forward(step).start()
            w_copy(0).wait_recv()
            for step in (1, 2, 3):
                w_forward(step).wait_recv()

        def step_of(order, carry, piece=piece):
            visit(order, piece, piece == PIECES - 1)
            return carry

        lax.fori_loop(0, orders, step_of, 0)
        finish(orders - 1, piece)

    def backward(index, carry):
        rows, columns = rows_columns(index)
        weights = attention[index]
        weights_bf = weights.astype(jnp.bfloat16)
        context_grad = grad_context[rows, columns].astype(jnp.bfloat16)
        gv_ref[rows, columns] = dot(weights_bf, context_grad, 0, 0).astype(jnp.bfloat16)
        attention_grad = dot(context_grad, v_ref[rows, columns], 1, 1)
        centred = jnp.sum(weights * attention_grad, axis=-1, keepdims=True)
        scores_grad = (weights * (attention_grad - centred) * scaling).astype(jnp.bfloat16)
        gq_ref[rows, columns] = dot(scores_grad, k_ref[rows, columns], 1, 0).astype(jnp.bfloat16)
        gk_ref[rows, columns] = dot(scores_grad, q_ref[rows, columns], 0, 0).astype(jnp.bfloat16)
        return carry

    lax.fori_loop(0, images * heads, backward, 0)
    stores = [
        pltpu.make_async_copy(gq_ref, gq_hbm, store.at[0]),
        pltpu.make_async_copy(gk_ref, gk_hbm, store.at[1]),
        pltpu.make_async_copy(gv_ref, gv_hbm, store.at[2]),
        pltpu.make_async_copy(gw_ref, gw_hbm, store.at[3]),
    ]
    for copy in stores[:3]:
        copy.start()

    for piece in range(PIECES):
        total = partial[chip, piece, core]
        for other in chips_at[1:]:
            block = sum_in.at[other, piece]
            remote(
                block, block, sum_send.at[other, piece], sum_recv.at[other, piece],
                2 * other + core, plane,
            ).wait_recv()
            total += sum_in[other, piece].astype(jnp.float32)
        gw_ref[piece * PIECE : (piece + 1) * PIECE, :] = total
    stores[3].start()

    for step in range(4):
        w_copy(step).wait_send()
        if step:
            w_forward(step).wait_send()

    def drain(index, carry):
        shard, piece = index // PIECES, index % PIECES
        pair_copy(shard, piece).wait_send()

        @pl.when(shard != chip)
        def _():
            sum_copy(shard, piece).wait_send()

        @pl.when(goes_up(shard))
        def _():
            up_copy(shard, piece).wait_send()

        @pl.when(goes_down(shard))
        def _():
            down_copy(shard, piece).wait_send()

        return carry

    lax.fori_loop(0, PLANES * PIECES, drain, 0)
    for copy in stores:
        copy.wait()


def place_kernel(*refs):
    for source, target in zip(refs[:4], refs[4:]):
        target[...] = source[...]


def fused_shards(query_heads, key_heads, value_heads, upstream, out_weight):
    tokens, width = query_heads.shape
    rows = out_weight.shape[0]
    heads = (tokens // PATCHES) * (width // HEAD)
    bf16, f32 = jnp.bfloat16, jnp.float32
    many = pltpu.SemaphoreType.DMA((PLANES, PIECES))
    few = pltpu.SemaphoreType.DMA((7,))
    piece_of = (PLANES, PIECES, PIECE, width)
    hbm = pl.BlockSpec(memory_space=pltpu.HBM)
    out_shape = [jax.ShapeDtypeStruct((tokens, width), bf16)] * 3
    out_shape += [jax.ShapeDtypeStruct((rows, width), f32)]
    grads = pl.pallas_call(
        fused_kernel,
        out_shape=out_shape,
        in_specs=[hbm] * 5,
        out_specs=[hbm] * 4,
        scratch_shapes=[pltpu.VMEM((tokens, width), bf16)] * 6
        + [pltpu.VMEM((rows, width), f32)]
        + [
            pltpu.VMEM((PLANES, PIECES, tokens, 2 * PIECE), bf16),
            pltpu.VMEM((CHIPS, PIECES, 2, PIECE, width), bf16),
            pltpu.VMEM((heads, PATCHES, PATCHES), f32),
            pltpu.VMEM((tokens, width), bf16),
            pltpu.VMEM((tokens, width), f32),
            pltpu.VMEM((PLANES, PIECES, 2, PIECE, width), f32),
            pltpu.VMEM(piece_of, bf16),
            pltpu.VMEM(piece_of, bf16),
            pltpu.VMEM(piece_of, bf16),
            pltpu.VMEM(piece_of, bf16),
        ]
        + [many] * 7
        + [few] * 2
        + [
            pltpu.SemaphoreType.DMA((PIECES, 2)),
            pltpu.SemaphoreType.DMA((4,)),
            pltpu.SemaphoreType.DMA((4,)),
        ],
        compiler_params=pltpu.CompilerParams(
            collective_id=0, has_side_effects=True, vmem_limit_bytes=56 * 2**20
        ),
        cost_estimate=pl.CostEstimate(
            flops=6_000_000_000, bytes_accessed=8_000_000, transcendentals=786_432
        ),
        name="fused",
    )(
        query_heads, key_heads, value_heads, upstream,
        out_weight.reshape(PIECES, PIECE, width),
    )
    steps = 2
    blocks = [pl.BlockSpec((tokens // steps, width), lambda step: (step, 0))] * 3
    blocks += [pl.BlockSpec((rows // steps, width), lambda step: (step, 0))]
    return pl.pallas_call(
        place_kernel,
        grid=(steps,),
        out_shape=out_shape,
        in_specs=blocks,
        out_specs=blocks,
        name="place",
    )(*grads)


def solution(mesh):
    fits = mesh.shape["dp"] == 2 * CHIPS and mesh.shape["mp"] == PLANES
    return jax.shard_map(
        fused_shards if fits else shards,
        mesh=mesh,
        in_specs=(P("dp", "mp"), P("dp", "mp"), P("dp", "mp"), P("dp", "mp"), P("dp", "mp")),
        out_specs=(P("dp", "mp"), P("dp", "mp"), P("dp", "mp"), P("dp", "mp")),
        check_vma=False,
    )
```

```python
import jax
import jax.numpy as jnp
from jax import lax
from jax.experimental import pallas as pl
from jax.experimental.pallas import tpu as pltpu
from jax.sharding import PartitionSpec as P

HEAD = 128
PATCHES = 256


def shards(query_heads, key_heads, value_heads, upstream, out_weight):
    tokens_here = query_heads.shape[0]
    local_width = query_heads.shape[1]
    upstream_full = lax.all_gather(upstream, "mp", axis=1, tiled=True)
    columns = upstream_full
    context_sum = jnp.dot(
        columns,
        lax.all_gather(out_weight, "dp", axis=0, tiled=True),
        preferred_element_type=jnp.float32,
    )
    grad_context = context_sum.astype(jnp.bfloat16)
    images_here = tokens_here // PATCHES
    scaling = HEAD ** (-0.5)

    def heads_of(tensor):
        return tensor.reshape(images_here, PATCHES, -1, HEAD)

    def rows_of(tensor):
        return tensor.reshape(tokens_here, local_width).astype(jnp.bfloat16)

    query_split = heads_of(query_heads)
    key_split = heads_of(key_heads)
    value_split = heads_of(value_heads)
    context_split = heads_of(grad_context)
    scores = (
        jnp.einsum("bqhd,bkhd->bhqk", query_split, key_split, preferred_element_type=jnp.float32)
        * scaling
    )
    attention = jax.nn.softmax(scores, axis=-1)
    weights_bf = attention.astype(jnp.bfloat16)
    context = rows_of(
        jnp.einsum("bhqk,bkhd->bqhd", weights_bf, value_split, preferred_element_type=jnp.float32)
    )
    columns = upstream_full
    grad_weight = lax.psum_scatter(
        lax.dot_general(
            columns, context, (((0,), (0,)), ((), ())), preferred_element_type=jnp.float32
        ),
        "dp",
        scatter_dimension=0,
        tiled=True,
    )
    grad_value = rows_of(
        jnp.einsum("bhqk,bqhd->bkhd", weights_bf, context_split, preferred_element_type=jnp.float32)
    )
    grad_attention = jnp.einsum(
        "bqhd,bkhd->bhqk", context_split, value_split, preferred_element_type=jnp.float32
    )
    centred = jnp.sum(attention * grad_attention, axis=-1, keepdims=True)
    grad_scores = (attention * (grad_attention - centred) * scaling).astype(jnp.bfloat16)
    grad_query = rows_of(
        jnp.einsum("bhqk,bkhd->bqhd", grad_scores, key_split, preferred_element_type=jnp.float32)
    )
    grad_key = rows_of(
        jnp.einsum("bhqk,bqhd->bkhd", grad_scores, query_split, preferred_element_type=jnp.float32)
    )
    return (grad_query, grad_key, grad_value, grad_weight)


MESH = pl.DeviceIdType.MESH
PLANES = 4
CHIPS = 4
PIECES = 3
PIECE = 128


def dot(left, right, left_dim, right_dim):
    return lax.dot_general(
        left, right, (((left_dim,), (right_dim,)), ((), ())), preferred_element_type=jnp.float32
    )


def fused_kernel(
    q_hbm, k_hbm, v_hbm, u_hbm, w_hbm,
    gq_hbm, gk_hbm, gv_hbm, gw_hbm,
    q_ref, k_ref, v_ref, gq_ref, gk_ref, gv_ref, gw_ref,
    u_all, w_all, attention, context, grad_context, partial, pair_out, pair_in, sum_out, sum_in,
    up_send, down_send, u_recv, pair_send, pair_recv, sum_send, sum_recv, w_send, w_recv, u_load, load, store,
):
    rank = lax.axis_index("dp")
    plane = lax.axis_index("mp")
    chip, core = rank // 2, rank % 2
    sibling = rank + 1 - 2 * core
    tokens, width = q_ref.shape
    heads = width // HEAD
    images = tokens // PATCHES
    scaling = HEAD ** (-0.5)
    chips_at = (chip, chip + 1 - 2 * (chip % 2), chip + 2 - 4 * (chip // 2), 3 - chip)

    def at(rank_there, plane_there):
        return {"dp": rank_there, "mp": plane_there}

    barrier = pltpu.get_barrier_semaphore()
    for rank_there in (sibling,) + tuple(2 * other + core for other in chips_at[1:]):
        pl.semaphore_signal(barrier, inc=1, device_id=at(rank_there, plane), device_id_type=MESH)
    for plane_there in ((plane + 1) % PLANES, (plane + PLANES - 1) % PLANES):
        pl.semaphore_signal(barrier, inc=1, device_id=at(rank, plane_there), device_id_type=MESH)

    def u_loads(piece):
        return [
            pltpu.make_async_copy(
                u_hbm.at[:, pl.ds((half * PIECES + piece) * PIECE, PIECE)],
                u_all.at[plane, piece, :, pl.ds(half * PIECE, PIECE)],
                u_load.at[piece, half],
            )
            for half in range(2)
        ]

    loads = [
        pltpu.make_async_copy(q_hbm, q_ref, load.at[0]),
        pltpu.make_async_copy(k_hbm, k_ref, load.at[1]),
        pltpu.make_async_copy(v_hbm, v_ref, load.at[2]),
        pltpu.make_async_copy(w_hbm, w_all.at[chip, :, core], load.at[3]),
    ]
    for piece in range(PIECES):
        for copy in u_loads(piece):
            copy.start()
    for copy in loads:
        copy.start()
    pl.semaphore_wait(barrier, 6)

    def remote(src, dst, send, recv, rank_there, plane_there):
        return pltpu.make_async_remote_copy(
            src_ref=src, dst_ref=dst, send_sem=send, recv_sem=recv,
            device_id=at(rank_there, plane_there), device_id_type=MESH,
        )

    def up_copy(shard, piece):
        block = u_all.at[shard, piece]
        return remote(
            block, block, up_send.at[shard, piece], u_recv.at[shard, piece], rank,
            (plane + 1) % PLANES,
        )

    def down_copy(shard, piece):
        block = u_all.at[shard, piece]
        return remote(
            block, block, down_send.at[shard, piece], u_recv.at[shard, piece], rank,
            (plane + PLANES - 1) % PLANES,
        )

    def goes_up(shard):
        return (plane < PLANES - 1) & (shard <= plane)

    def goes_down(shard):
        return (plane > 0) & (shard >= plane)

    def send_on(shard, piece):
        @pl.when(goes_up(shard))
        def _():
            up_copy(shard, piece).start()

        @pl.when(goes_down(shard))
        def _():
            down_copy(shard, piece).start()

    for copy in u_loads(0):
        copy.wait()
    send_on(plane, 0)

    def w_copy(step):
        if step == 0:
            return remote(
                w_hbm, w_all.at[chip, :, core], w_send.at[0], w_recv.at[0], sibling, plane
            )
        return remote(
            w_hbm, w_all.at[chip, :, core], w_send.at[step], w_recv.at[step],
            2 * chips_at[step] + core, plane,
        )

    def w_forward(step):
        block = w_all.at[chips_at[step], :, core]
        return remote(block, block, w_send.at[3 + step], w_recv.at[3 + step], sibling, plane)

    for step in (1, 2, 3, 0):
        w_copy(step).start()
    for piece in range(1, PIECES):
        for copy in u_loads(piece):
            copy.wait()
        send_on(plane, piece)
    for copy in loads:
        copy.wait()

    def rows_columns(index):
        rows = pl.ds(pl.multiple_of((index // heads) * PATCHES, PATCHES), PATCHES)
        columns = pl.ds(pl.multiple_of((index % heads) * HEAD, HEAD), HEAD)
        return rows, columns

    def forward(index, carry):
        rows, columns = rows_columns(index)
        scores = dot(q_ref[rows, columns], k_ref[rows, columns], 1, 1) * scaling
        raised = jnp.exp(scores - jnp.max(scores, axis=-1, keepdims=True))
        weights = raised / jnp.sum(raised, axis=-1, keepdims=True)
        attention[index] = weights
        context[rows, columns] = dot(
            weights.astype(jnp.bfloat16), v_ref[rows, columns], 1, 0
        ).astype(jnp.bfloat16)
        return carry

    lax.fori_loop(0, images * heads, forward, 0)

    def pair_copy(shard, piece):
        return remote(
            pair_out.at[shard, piece], pair_in.at[shard, piece], pair_send.at[shard, piece],
            pair_recv.at[shard, piece], sibling, plane,
        )

    def sum_copy(shard, piece):
        return remote(
            sum_out.at[shard, piece], sum_in.at[chip, piece], sum_send.at[shard, piece],
            sum_recv.at[chip, piece], 2 * shard + core, plane,
        )

    def shard_of(order):
        distance = (order + 1) // 2
        shard = plane + distance * (1 - 2 * (order % 2))
        return shard, (shard >= 0) & (shard < PLANES)

    def finish(order, piece):
        shard, valid = shard_of(order)

        @pl.when(valid)
        def _():
            pair_copy(shard, piece).wait_recv()

            @pl.when(shard == chip)
            def _():
                partial[shard, piece, core] += pair_in[shard, piece].astype(jnp.float32)

            @pl.when(shard != chip)
            def _():
                total = partial[shard, piece, core] + pair_in[shard, piece].astype(jnp.float32)
                sum_out[shard, piece] = total.astype(jnp.bfloat16)
                sum_copy(shard, piece).start()

    def visit(order, piece, last):
        shard, valid = shard_of(order)

        @pl.when(valid)
        def _():
            @pl.when(order > 0)
            def _():
                up_copy(shard, piece).wait_recv()
                send_on(shard, piece)

        @pl.when(order > 0)
        def _():
            finish(order - 1, piece)

        if last:
            @pl.when(order == 4)
            def _():
                for step in (1, 2, 3):
                    w_copy(step).wait_recv()
                    w_forward(step).start()

        @pl.when(valid)
        def _():
            for tile in range(width // 256):
                columns = slice(tile * 256, (tile + 1) * 256)
                product = dot(u_all[shard, piece], context[:, columns], 0, 0)
                partial[shard, piece, :, :, columns] = product.reshape(2, PIECE, 256)
            pair_out[shard, piece] = partial[shard, piece, 1 - core].astype(jnp.bfloat16)
            pair_copy(shard, piece).start()

    orders = 2 * PLANES - 1
    for piece in range(PIECES):
        def step_of(order, carry, piece=piece):
            visit(order, piece, piece == PIECES - 1)
            return carry

        lax.fori_loop(0, orders, step_of, 0)
        finish(orders - 1, piece)

    def backward(index, carry):
        rows, columns = rows_columns(index)
        weights = attention[index]
        weights_bf = weights.astype(jnp.bfloat16)
        context_grad = grad_context[rows, columns].astype(jnp.bfloat16)
        gv_ref[rows, columns] = dot(weights_bf, context_grad, 0, 0).astype(jnp.bfloat16)
        attention_grad = dot(context_grad, v_ref[rows, columns], 1, 1)
        centred = jnp.sum(weights * attention_grad, axis=-1, keepdims=True)
        scores_grad = (weights * (attention_grad - centred) * scaling).astype(jnp.bfloat16)
        gq_ref[rows, columns] = dot(scores_grad, k_ref[rows, columns], 1, 0).astype(jnp.bfloat16)
        gk_ref[rows, columns] = dot(scores_grad, q_ref[rows, columns], 0, 0).astype(jnp.bfloat16)
        return carry

    w_copy(0).wait_recv()
    for step in (1, 2, 3):
        w_forward(step).wait_recv()

    def project(tile, carry):
        columns = pl.ds(pl.multiple_of(tile * 256, 256), 256)
        total = jnp.zeros((tokens, 256), jnp.float32)
        for shard in range(PLANES):
            for part in range(PIECES):
                rows = w_all[shard, part, :, :, columns].reshape(2 * PIECE, 256)
                total += dot(u_all[shard, part], rows, 1, 0)
        grad_context[:, columns] = total
        return carry

    lax.fori_loop(0, width // 256, project, 0)
    lax.fori_loop(0, images * heads, backward, 0)
    stores = [
        pltpu.make_async_copy(gq_ref, gq_hbm, store.at[0]),
        pltpu.make_async_copy(gk_ref, gk_hbm, store.at[1]),
        pltpu.make_async_copy(gv_ref, gv_hbm, store.at[2]),
        pltpu.make_async_copy(gw_ref, gw_hbm, store.at[3]),
    ]
    for copy in stores[:3]:
        copy.start()

    for piece in range(PIECES):
        total = partial[chip, piece, core]
        for other in chips_at[1:]:
            block = sum_in.at[other, piece]
            remote(
                block, block, sum_send.at[other, piece], sum_recv.at[other, piece],
                2 * other + core, plane,
            ).wait_recv()
            total += sum_in[other, piece].astype(jnp.float32)
        gw_ref[piece * PIECE : (piece + 1) * PIECE, :] = total
    stores[3].start()

    for step in range(4):
        w_copy(step).wait_send()
        if step:
            w_forward(step).wait_send()

    def drain(index, carry):
        shard, piece = index // PIECES, index % PIECES
        pair_copy(shard, piece).wait_send()

        @pl.when(shard != chip)
        def _():
            sum_copy(shard, piece).wait_send()

        @pl.when(goes_up(shard))
        def _():
            up_copy(shard, piece).wait_send()

        @pl.when(goes_down(shard))
        def _():
            down_copy(shard, piece).wait_send()

        return carry

    lax.fori_loop(0, PLANES * PIECES, drain, 0)
    for copy in stores:
        copy.wait()


def place_kernel(*refs):
    for source, target in zip(refs[:4], refs[4:]):
        target[...] = source[...]


def fused_shards(query_heads, key_heads, value_heads, upstream, out_weight):
    tokens, width = query_heads.shape
    rows = out_weight.shape[0]
    heads = (tokens // PATCHES) * (width // HEAD)
    bf16, f32 = jnp.bfloat16, jnp.float32
    many = pltpu.SemaphoreType.DMA((PLANES, PIECES))
    few = pltpu.SemaphoreType.DMA((7,))
    piece_of = (PLANES, PIECES, PIECE, width)
    hbm = pl.BlockSpec(memory_space=pltpu.HBM)
    out_shape = [jax.ShapeDtypeStruct((tokens, width), bf16)] * 3
    out_shape += [jax.ShapeDtypeStruct((rows, width), f32)]
    grads = pl.pallas_call(
        fused_kernel,
        out_shape=out_shape,
        in_specs=[hbm] * 5,
        out_specs=[hbm] * 4,
        scratch_shapes=[pltpu.VMEM((tokens, width), bf16)] * 6
        + [pltpu.VMEM((rows, width), f32)]
        + [
            pltpu.VMEM((PLANES, PIECES, tokens, 2 * PIECE), bf16),
            pltpu.VMEM((CHIPS, PIECES, 2, PIECE, width), bf16),
            pltpu.VMEM((heads, PATCHES, PATCHES), f32),
            pltpu.VMEM((tokens, width), bf16),
            pltpu.VMEM((tokens, width), f32),
            pltpu.VMEM((PLANES, PIECES, 2, PIECE, width), f32),
            pltpu.VMEM(piece_of, bf16),
            pltpu.VMEM(piece_of, bf16),
            pltpu.VMEM(piece_of, bf16),
            pltpu.VMEM(piece_of, bf16),
        ]
        + [many] * 7
        + [few] * 2
        + [
            pltpu.SemaphoreType.DMA((PIECES, 2)),
            pltpu.SemaphoreType.DMA((4,)),
            pltpu.SemaphoreType.DMA((4,)),
        ],
        compiler_params=pltpu.CompilerParams(
            collective_id=0, has_side_effects=True, vmem_limit_bytes=56 * 2**20
        ),
        cost_estimate=pl.CostEstimate(
            flops=6_000_000_000, bytes_accessed=8_000_000, transcendentals=786_432
        ),
        name="fused",
    )(
        query_heads, key_heads, value_heads, upstream,
        out_weight.reshape(PIECES, PIECE, width),
    )
    steps = 2
    blocks = [pl.BlockSpec((tokens // steps, width), lambda step: (step, 0))] * 3
    blocks += [pl.BlockSpec((rows // steps, width), lambda step: (step, 0))]
    return pl.pallas_call(
        place_kernel,
        grid=(steps,),
        out_shape=out_shape,
        in_specs=blocks,
        out_specs=blocks,
        name="place",
    )(*grads)


def solution(mesh):
    fits = mesh.shape["dp"] == 2 * CHIPS and mesh.shape["mp"] == PLANES
    return jax.shard_map(
        fused_shards if fits else shards,
        mesh=mesh,
        in_specs=(P("dp", "mp"), P("dp", "mp"), P("dp", "mp"), P("dp", "mp"), P("dp", "mp")),
        out_specs=(P("dp", "mp"), P("dp", "mp"), P("dp", "mp"), P("dp", "mp")),
        check_vma=False,
    )
```
